32 devices in a mesh: groups: 2 (over y), expert: 4 (over z), tensor: 2 (over x), dp: 2 (over core).
Axes of the slice: x: 2, y: 2, z: 4, core: 2. Of those that a mesh axis runs over, the one named last changes fastest.
Arguments:
- inputs: bfloat16 [2, 256, 3584], P(None, ('groups', 'expert', 'dp')), parts along dimension 1, may hold values from -6 to 6
- attn_gain: float32 [3584], replicated, may hold values from 0.1 to 1.9
- qkv_weight: bfloat16 [3584, 512], P('tensor'), may hold values from -0.09375 to 0.09375
- out_weight: bfloat16 [256, 3584], P(None, 'tensor'), may hold values from -0.375 to 0.375
- cache: bfloat16 [256, 256, 256], P(('groups', 'expert', 'dp'), 'tensor'), parts along dimension 0, may hold values from -240 to 240
- lengths: int32 [256], P(('groups', 'expert', 'dp')), parts along dimension 0, may hold values from 1 to 256, as said below
- moe_gain: float32 [3584], replicated, may hold values from 0.1 to 1.9
- router_weight: bfloat16 [3584, 16], replicated, may hold values from -0.09375 to 0.09375
- expert_ids: int32 [2, 256, 8], P(None, ('groups', 'expert', 'dp')), parts along dimension 1, may hold values from 0 to 15, all different within a row; in each aligned block of 16 rows (0 to 15, 16 to 31, ..., all dimensions but the last counted through in order) at most 15 rows name the same one
- gate_weight: bfloat16 [16, 3584, 1024], P('expert', 'tensor'), may hold values from -0.09375 to 0.09375
- up_weight: bfloat16 [16, 3584, 1024], P('expert', 'tensor'), may hold values from -0.09375 to 0.09375
- down_weight: bfloat16 [16, 1024, 3584], P('expert', None, 'tensor'), may hold values from -0.1875 to 0.1875
- pool_left: bfloat16 [64, 2, 3584, 64], P(('groups', 'expert'), None, 'tensor'), parts along dimension 0, may hold values from -0.75 to 0.75
- pool_right: bfloat16 [64, 2, 64, 1024], P(('groups', 'expert'), None, None, 'dp'), parts along dimension 0, may hold values from -0.09375 to 0.09375
- pair_slot: int32 [32], P('groups'), parts along dimension 0, may hold values from 0 to 31, as said below
Outputs:
- outputs: bfloat16 [2, 256, 3584], P(None, ('groups', 'expert', 'dp'), 'tensor'), parts along dimension 1
The draws below stay inside these ranges and needn't reach their ends.
There are 2 independent parts, one for each index of `groups`. The reference program is written for one: setup_inputs(seed, part) draws one part's arguments, and reference() takes and returns one part's arrays. A program takes and returns all parts, laid end to end along the dimension named above; an argument that names none is the same for every part. Nothing has to cross between parts.
Inputs may be any that keep to these rules, and one draw needn't show every extreme that they name: `expert_ids`: each row names 8 different experts; in the rows of one device at one step (aligned blocks of 16 rows) no expert is named by more than 15 rows, a bound that some block reaches. `pair_slot`: slot j lies on trainer shard j // 8; no slot holds two experts; some trainer shard holds 8 experts. `lengths`: some row has length 256.
All inputs are finite; a program needn't handle non-finite values.
Results may differ from the reference program's by a relative error of at most 0.015.
The reference program's roundings to bfloat16 on the way count: a program that leaves them out, or rounds other values in their place, can miss the bound.
Values may be sent and summed in bfloat16 or wider, within the bound.
A program may use at most 192 MiB of HBM per device.

```python
import math
import jax
import jax.numpy as jnp
import numpy as np
from jax import lax

D = 3584
FFW = 1024
LAT = 256
RANK = 64
EXPERTS = 16
TOP = 8
STEPS = 2
ROWS_DEV = 16
L = 256
CAP = 15
SLOTS = 8
POOL = 32
ROWS = 128


def draw_cache(key, part):
    key = jax.random.fold_in(key, 11)
    value_key = jax.random.fold_in(key, 0)
    values = jnp.clip(jax.random.normal(value_key, (ROWS, L, LAT), jnp.float32), -6.0, 6.0)
    return values.astype(jnp.bfloat16)


def draw_lengths(key, part):
    key = jax.random.fold_in(key, 12)
    length_key, longest_key = jax.random.split(key)
    lengths_drawn = jax.random.randint(length_key, (ROWS,), 1, L + 1, jnp.int32)
    longest = jax.random.randint(longest_key, (), 0, ROWS, jnp.int32)
    return jnp.where(jnp.arange(ROWS, dtype=jnp.int32) == longest, L, lengths_drawn).astype(jnp.int32)


def draw_pair_slot(key, part):
    key = jax.random.fold_in(key, 13)
    shard_key, rest_key, mix_key = jax.random.split(key, 3)
    slot_total = 2 * EXPERTS
    shards = slot_total // SLOTS
    crowded = jax.random.randint(shard_key, (), 0, shards, jnp.int32)
    others = jax.random.permutation(rest_key, slot_total - SLOTS).astype(jnp.int32)
    others = jnp.where(others >= crowded * SLOTS, others + SLOTS, others)
    listed = jnp.concatenate([crowded * SLOTS + jnp.arange(SLOTS, dtype=jnp.int32), others])[:EXPERTS]
    shuffled = jax.random.permutation(mix_key, EXPERTS)
    return listed[shuffled].astype(jnp.int32)


def block_scale(stream_key, shape, cuts, smallest, largest):
    factor_of, own = 1.0, jax.random.fold_in(stream_key, 6)
    for axis_at, shards_of in cuts:
        draws = jnp.exp(jax.random.uniform(jax.random.fold_in(own, axis_at), (shards_of,), jnp.float32, smallest / len(cuts), largest / len(cuts)))
        factor_of = factor_of * jnp.repeat(draws, shape[axis_at] // shards_of).reshape([-1 if axis == axis_at else 1 for axis in range(len(shape))])
    return factor_of


def deal_out(rng, own, number, rows, amount, top, most, skew):
    ranking = jax.random.permutation(rng, amount)
    crowded, common = load_shares(amount, rows * top, most, skew, True), load_shares(amount, rows * top, most, skew, False)
    places = jnp.arange(amount)

    def named(tallies, offset_by):
        used = int((tallies > 0).sum())
        fixed = max(1, used // 4)
        moved = fixed + (places - fixed + offset_by * (used - fixed)) % max(1, amount - fixed)
        return jnp.zeros((amount,), jnp.int32).at[ranking[jnp.where(places < fixed, places, moved)]].set(jnp.asarray(tallies, jnp.int32))

    tallies = jnp.where(number % 4 == 0, named(crowded, number // 4), named(common, number - number // 4 - 1))
    mixed = jax.random.permutation(jax.random.fold_in(own, 3), amount)
    source_of, receiver = mixed[0:amount // 2 * 2:2], mixed[1:amount // 2 * 2:2]
    margin = jnp.minimum(tallies[source_of] - 1, most - tallies[receiver]) // 2
    margin = jnp.where((source_of == ranking[0]) | (receiver == ranking[0]) | (tallies[receiver] == 0), 0, jnp.maximum(margin, 0))
    moved = jax.random.randint(jax.random.fold_in(own, 4), (amount // 2,), 0, 1 << 20) % (margin + 1)
    tallies = tallies.at[source_of].add(-moved).at[receiver].add(moved)
    items = jnp.searchsorted(jnp.cumsum(tallies), jnp.arange(rows * top), side="right").astype(jnp.int32)
    grid = items.reshape(top, rows).T
    grid = grid[jax.random.permutation(jax.random.fold_in(own, 1), rows)]
    offset_by = jax.random.randint(jax.random.fold_in(own, 2), (rows, 1), 0, top)
    return jnp.take_along_axis(grid, (jnp.arange(top)[None, :] + offset_by) % top, axis=1)


def load_shares(count, total, reach, slope, full):
    weights = [(1 << 20) // math.isqrt(standing ** slope) + 1 for standing in range(1, count + 1)]
    largest = reach if full else min(reach, max(-(-total // count), total * weights[0] // sum(weights)))
    least = 1 if total - largest >= count - 1 else 0
    holding, rest = [largest] + [least] * (count - 1), total - largest - least * (count - 1)
    while rest > 0:
        candidates = [i for i in range(1, count) if holding[i] < largest] or [i for i in range(1, count) if holding[i] < reach]
        whole, left = sum([weights[i] for i in candidates]), rest
        for i in candidates:
            extra = min(reach - holding[i], max(1, left * weights[i] // whole), rest)
            holding[i] = holding[i] + extra
            rest = rest - extra
    return np.array(holding)


def bell_draw(key, shape, scale, bound, cuts=(), held_as=jnp.bfloat16):
    loudness = block_scale(key, shape, cuts, -0.22, 0.18) if cuts else 1.0
    entries = jax.random.normal(key, shape, jnp.float32) * scale * loudness
    return jnp.minimum(jnp.maximum(entries, -bound), bound).astype(held_as)


def setup_inputs(seed: int = 0, part: int = 0) -> dict:
    key_of = jax.random.split(jax.random.key(seed), 16)
    part_keys = jax.random.split(jax.random.fold_in(key_of[15], part), 16)
    inputs = bell_draw(part_keys[0], (STEPS, ROWS, D), 1.0, 6.0, ((1, 8),))
    attn_gain = jnp.clip(1.0 + 0.18 * jax.random.normal(key_of[1], (D,), jnp.float32), 0.1, 1.9)
    qkv_weight = bell_draw(key_of[2], (D, 2 * LAT), D ** -0.5, 0.09375, ((0, 2),))
    out_weight = bell_draw(key_of[3], (LAT, D), LAT ** -0.5, 0.375, ((1, 2),))
    cache = draw_cache(jax.random.fold_in(jax.random.fold_in(key_of[15], part), 71), part)
    lengths = draw_lengths(jax.random.fold_in(jax.random.fold_in(key_of[15], part), 71), part)
    moe_gain = jnp.clip(1.0 + 0.18 * jax.random.normal(key_of[6], (D,), jnp.float32), 0.1, 1.9)
    router_weight = bell_draw(key_of[7], (D, EXPERTS), D ** -0.5, 0.09375)
    expert_ids_keys = jax.random.split(jax.random.fold_in(part_keys[8], 1), STEPS * ROWS // ROWS_DEV)
    expert_ids_turns = jax.random.permutation(jax.random.fold_in(part_keys[8], 3), STEPS * ROWS // ROWS_DEV)
    expert_ids = jax.vmap(lambda own, number: deal_out(jax.random.fold_in(part_keys[8], 2), own, number, ROWS_DEV, EXPERTS, TOP, CAP, 2))(expert_ids_keys, expert_ids_turns).reshape((STEPS, ROWS, TOP))
    gate_weight = bell_draw(key_of[9], (EXPERTS, D, FFW), D ** -0.5, 0.09375, ((0, 4), (1, 2)))
    up_weight = bell_draw(key_of[10], (EXPERTS, D, FFW), D ** -0.5, 0.09375, ((0, 4), (1, 2)))
    down_weight = bell_draw(key_of[11], (EXPERTS, FFW, D), FFW ** -0.5, 0.1875, ((0, 4), (2, 2)))
    pool_left = bell_draw(part_keys[12], (POOL, 2, D, RANK), RANK ** -0.5, 0.75, ((0, 4), (2, 2)))
    pool_right = bell_draw(part_keys[13], (POOL, 2, RANK, FFW), D ** -0.5, 0.09375, ((0, 4), (3, 2)))
    pair_slot = draw_pair_slot(jax.random.fold_in(jax.random.fold_in(key_of[15], part), 71), part)
    return {"inputs": inputs, "attn_gain": attn_gain, "qkv_weight": qkv_weight, "out_weight": out_weight, "cache": cache, "lengths": lengths, "moe_gain": moe_gain, "router_weight": router_weight, "expert_ids": expert_ids, "gate_weight": gate_weight, "up_weight": up_weight, "down_weight": down_weight, "pool_left": pool_left, "pool_right": pool_right, "pair_slot": pair_slot}


EPS = 1e-06
ROUTE_SCALE = 2.5

def normalized(values, norm_gain):
    widened = values.astype(jnp.float32)
    square_mean = lax.optimization_barrier(jnp.mean(widened * widened, axis=-1, keepdims=True))
    return (widened * lax.rsqrt(square_mean + EPS) * norm_gain).astype(jnp.bfloat16)

def merged_weights(gate_weight, up_weight, left_rows, right_rows):

    def single(bundle):
        gate_one, up_one, left_one, right_one = bundle
        gate_new = gate_one.astype(jnp.float32) + jnp.dot(left_one[0], right_one[0], preferred_element_type=jnp.float32)
        up_new = up_one.astype(jnp.float32) + jnp.dot(left_one[1], right_one[1], preferred_element_type=jnp.float32)
        return (gate_new.astype(jnp.bfloat16), up_new.astype(jnp.bfloat16))
    return lax.map(single, (gate_weight, up_weight, left_rows, right_rows))

def attend_block(bundle):
    queries, cached_keys, limits, recent = bundle
    score_scale = LAT ** (-0.5)
    query_wide = queries.astype(jnp.float32)
    keys_wide = cached_keys.astype(jnp.float32)
    recent_wide = recent.astype(jnp.float32)
    visible = jnp.arange(L, dtype=jnp.int32)[None, :] < limits[:, None]
    cached = jnp.einsum('bl,bpl->bp', query_wide, keys_wide, precision=lax.Precision.HIGHEST) * score_scale
    cached = jnp.where(visible, cached, -jnp.inf)
    latest = jnp.einsum('bl,bkl->bk', query_wide, recent_wide, precision=lax.Precision.HIGHEST) * score_scale
    highest = jnp.maximum(lax.optimization_barrier(jnp.max(cached, axis=-1)), lax.optimization_barrier(jnp.max(latest, axis=-1)))
    cached_weights = jnp.where(visible, jnp.exp(cached - highest[:, None]), 0.0)
    latest_weights = jnp.exp(latest - highest[:, None])
    denominator = lax.optimization_barrier(jnp.sum(cached_weights, axis=-1)) + lax.optimization_barrier(jnp.sum(latest_weights, axis=-1))
    summed = jnp.einsum('bp,bpl->bl', cached_weights, keys_wide, precision=lax.Precision.HIGHEST)
    summed = summed + jnp.einsum('bk,bkl->bl', latest_weights, recent_wide, precision=lax.Precision.HIGHEST)
    return (summed / denominator[:, None]).astype(jnp.bfloat16)

def reference(inputs, attn_gain, qkv_weight, out_weight, cache, lengths, moe_gain, router_weight, expert_ids, gate_weight, up_weight, down_weight, pool_left, pool_right, pair_slot):
    left_rows = jnp.take(pool_left, pair_slot, axis=0)
    right_rows = jnp.take(pool_right, pair_slot, axis=0)
    gate_merged, up_merged = merged_weights(gate_weight, up_weight, left_rows, right_rows)
    blocks = ROWS // ROWS_DEV
    fresh_keys = []
    results = []
    for step_index in range(STEPS):
        tokens = inputs[step_index]
        normed = normalized(tokens, attn_gain)
        projected = jnp.dot(normed, qkv_weight, preferred_element_type=jnp.float32)
        queries = projected[:, :LAT].astype(jnp.bfloat16)
        fresh_keys.append(projected[:, LAT:].astype(jnp.bfloat16))
        recent = jnp.stack(fresh_keys, axis=1)
        attended = lax.map(attend_block, (queries.reshape(blocks, ROWS_DEV, LAT), cache.reshape(blocks, ROWS_DEV, L, LAT), lengths.reshape(blocks, ROWS_DEV), recent.reshape(blocks, ROWS_DEV, step_index + 1, LAT)))
        attended = attended.reshape(ROWS, LAT)
        middle = (tokens.astype(jnp.float32) + jnp.dot(attended, out_weight, preferred_element_type=jnp.float32)).astype(jnp.bfloat16)
        middle_wide = middle.astype(jnp.float32)
        square_mean = lax.optimization_barrier(jnp.mean(middle_wide * middle_wide, axis=-1))
        inverse = lax.rsqrt(square_mean + EPS)
        routed_in = (middle_wide * inverse[:, None] * moe_gain).astype(jnp.bfloat16)
        logits = inverse[:, None] * jnp.dot(middle_wide * moe_gain, router_weight.astype(jnp.float32), precision=lax.Precision.HIGHEST)
        routes_now = expert_ids[step_index]
        picked = jnp.take_along_axis(logits, routes_now, axis=1)
        gated_scores = jax.nn.sigmoid(picked)
        route_weights = (ROUTE_SCALE * gated_scores / lax.optimization_barrier(jnp.sum(gated_scores, axis=-1, keepdims=True))).astype(jnp.bfloat16)

        def expert_step(running, bundle):
            expert, gate_one, up_one, down_one = bundle
            gate_pre = jnp.dot(routed_in, gate_one, preferred_element_type=jnp.float32)
            up_pre = jnp.dot(routed_in, up_one, preferred_element_type=jnp.float32)
            hidden = (jax.nn.silu(gate_pre) * up_pre).astype(jnp.bfloat16)
            output = jnp.dot(hidden, down_one, preferred_element_type=jnp.float32).astype(jnp.bfloat16)
            weight_sum = lax.optimization_barrier(jnp.sum(jnp.where(routes_now == expert, route_weights.astype(jnp.float32), 0.0), axis=-1))
            return (running + weight_sum[:, None] * output.astype(jnp.float32), None)
        mixture, _ = lax.scan(expert_step, jnp.zeros((ROWS, D), jnp.float32), (jnp.arange(EXPERTS, dtype=jnp.int32), gate_merged, up_merged, down_weight))
        results.append((middle_wide + mixture).astype(jnp.bfloat16))
    return jnp.stack(results, axis=0)
```

```python
import jax
import jax.numpy as jnp
from jax import lax
from jax.sharding import PartitionSpec as P

EPS = 1e-06
ROUTE_SCALE = 2.5
FLOOR = -1e30
F32 = jnp.float32
BF16 = jnp.bfloat16


def split_terms(value, count):
    terms = []
    for _ in range(count):
        term = lax.reduce_precision(value, 8, 7)
        terms.append(term.astype(BF16))
        value = value - term
    return terms


def shards(
    inputs,
    attn_gain,
    qkv_weight,
    out_weight,
    cache,
    lengths,
    moe_gain,
    router_weight,
    expert_ids,
    gate_weight,
    up_weight,
    down_weight,
    pool_left,
    pool_right,
    pair_slot,
):
    steps, rows_here, width = inputs.shape
    experts_here, part_cols, ffw = gate_weight.shape
    slots_here, _, _, rank = pool_left.shape
    right_cols = pool_right.shape[3]
    lat = cache.shape[2]
    span_here = cache.shape[1]
    shard_count = lax.axis_size("expert")
    shard_index = lax.axis_index("expert")
    tensor_count = lax.axis_size("tensor")
    tensor_index = lax.axis_index("tensor")
    expert_count = shard_count * experts_here
    col_start = tensor_index * part_cols
    batch = steps * rows_here
    total_rows = shard_count * batch
    score_scale = lat ** (-0.5)
    paired = tensor_count == 2

    own_slots = shard_index * slots_here + jnp.arange(slots_here, dtype=jnp.int32)
    serves = (pair_slot[:, None] == own_slots[None, :]).astype(BF16)

    piece_cols = right_cols // tensor_count
    right_piece = lax.dynamic_slice_in_dim(pool_right, tensor_index * piece_cols, piece_cols, 3)
    right_sent = jnp.einsum(
        "es,sxrf->exrf", serves, right_piece, preferred_element_type=F32
    ).astype(BF16)
    right_sent = right_sent.reshape(shard_count, experts_here, 2, rank, piece_cols)
    right_got = lax.all_to_all(right_sent, "expert", split_axis=0, concat_axis=0, tiled=True)
    right_own = jnp.sum(right_got.astype(F32), axis=0).astype(BF16)
    right_full = lax.all_gather(right_own, ("dp", "tensor"), axis=3, tiled=True)

    chosen = jnp.any(
        expert_ids.reshape(batch, -1)[:, :, None]
        == jnp.arange(expert_count, dtype=jnp.int32)[None, None, :],
        axis=1,
    ).astype(BF16)
    chosen_all = lax.all_gather(chosen, "expert", axis=0, tiled=False)

    tokens = inputs.reshape(batch, width)
    tokens_wide = tokens.astype(F32)
    square_mean = jnp.mean(tokens_wide * tokens_wide, axis=-1, keepdims=True)
    token_cols = lax.dynamic_slice_in_dim(tokens, col_start, part_cols, 1)
    gain_piece = lax.dynamic_slice_in_dim(attn_gain, col_start, part_cols, 0)
    normed_cols = (
        token_cols.astype(F32) * lax.rsqrt(square_mean + EPS) * gain_piece
    ).astype(BF16)
    projected = lax.psum(jnp.dot(normed_cols, qkv_weight, preferred_element_type=F32), "tensor")
    queries = projected[:, :lat].astype(BF16).reshape(steps, rows_here, lat)
    fresh = projected[:, lat:].astype(BF16).reshape(steps, rows_here, lat)

    positions = tensor_index * span_here + jnp.arange(span_here, dtype=jnp.int32)
    visible = (positions[None, :] < lengths[:, None])[:, None, :]
    scores = (
        jnp.einsum("sbl,bpl->bsp", queries, cache, preferred_element_type=F32) * score_scale
    )
    local_top = jnp.max(jnp.where(visible, scores, FLOOR), axis=-1, keepdims=True)
    weights = jnp.where(visible, jnp.exp(scores - local_top), 0.0)
    terms = jnp.concatenate(split_terms(weights, 3), axis=1)
    sums = jnp.einsum("bmp,bpl->bml", terms, cache, preferred_element_type=F32)
    sums = jnp.sum(sums.reshape(rows_here, 3, steps, lat), axis=1)
    local_total = jnp.sum(weights, axis=-1, keepdims=True)
    packed = jnp.concatenate(
        (
            sums,
            jnp.broadcast_to(local_top, (rows_here, steps, 64)),
            jnp.broadcast_to(local_total, (rows_here, steps, 64)),
        ),
        axis=2,
    )
    parts = lax.all_gather(packed, "tensor", axis=0, tiled=False)
    part_sums, part_tops, part_totals = (
        parts[..., :lat],
        parts[..., lat],
        parts[..., lat + 64],
    )

    fresh_wide = fresh.astype(F32)
    latest = (
        jnp.sum(queries.astype(F32)[:, None] * fresh_wide[None], axis=-1) * score_scale
    )
    step_range = jnp.arange(steps)
    usable = (step_range[None, :] <= step_range[:, None])[:, :, None]
    latest_top = jnp.max(jnp.where(usable, latest, FLOOR), axis=1)
    highest = jnp.maximum(jnp.max(part_tops, axis=0), latest_top.T)
    factors = jnp.exp(part_tops - highest[None])
    latest_weights = jnp.where(usable, jnp.exp(latest - highest.T[:, None, :]), 0.0)
    denominator = jnp.sum(part_totals * factors, axis=0) + jnp.sum(latest_weights, axis=1).T
    numerator = jnp.sum(part_sums * factors[..., None], axis=0).transpose(1, 0, 2) + jnp.sum(
        latest_weights[..., None] * fresh_wide[None], axis=1
    )
    attended = (numerator / denominator.T[..., None]).astype(BF16).reshape(batch, lat)
    middle = (
        token_cols.astype(F32) + jnp.dot(attended, out_weight, preferred_element_type=F32)
    ).astype(BF16)

    gain_cols = lax.dynamic_slice_in_dim(moe_gain, col_start, part_cols, 0)
    router_rows = lax.dynamic_slice_in_dim(router_weight, col_start, part_cols, 0).astype(F32)
    middle_wide = middle.astype(F32)
    partial_logits = jnp.dot(
        middle_wide * gain_cols, router_rows, precision=lax.Precision.HIGHEST
    )
    partial_squares = jnp.sum(middle_wide * middle_wide, axis=-1, keepdims=True)
    statistics = jnp.concatenate(
        (partial_logits, jnp.broadcast_to(partial_squares, (batch, 128 - expert_count))), axis=1
    )
    statistics = lax.all_gather(statistics, ("expert", "tensor"), axis=0, tiled=False)
    statistics = jnp.sum(
        statistics.reshape(shard_count, tensor_count, batch, 128), axis=1
    )
    middle_all = lax.all_gather(middle, "expert", axis=0, tiled=False)

    def turned(value):
        if not paired:
            return value
        half = shard_count // 2
        swapped = jnp.concatenate((value[half:], value[:half]), axis=0)
        return jnp.where(tensor_index == 0, value, swapped)

    statistics = turned(statistics).reshape(total_rows, 128)
    rows_all = turned(middle_all).reshape(total_rows, part_cols)
    mask_all = turned(chosen_all).reshape(total_rows, expert_count).astype(F32)

    inverse = lax.rsqrt(statistics[:, 127:] / width + EPS)
    routed_in = (rows_all.astype(F32) * inverse * gain_cols).astype(BF16)
    gated = jax.nn.sigmoid(inverse * statistics[:, :expert_count]) * mask_all
    route = (ROUTE_SCALE * gated / jnp.sum(gated, axis=-1, keepdims=True)).astype(BF16)
    route_here = lax.dynamic_slice_in_dim(
        route, shard_index * experts_here, experts_here, 1
    ).astype(F32)

    low = jnp.einsum("nd,sxdr->sxnr", routed_in, pool_left, preferred_element_type=F32)
    low_sent = jnp.einsum(
        "es,sxnr->exnr", serves, low.astype(BF16), preferred_element_type=F32
    ).astype(BF16)
    low_sent = low_sent.reshape(shard_count, experts_here, 2, total_rows, rank)
    low_got = lax.all_to_all(low_sent, "expert", split_axis=0, concat_axis=0, tiled=True)
    low_own = jnp.sum(low_got.astype(F32), axis=0).astype(BF16)

    exchange = [(0, 1), (1, 0)]
    mixture = jnp.zeros((total_rows, part_cols), F32)
    for expert in range(experts_here):
        partial = [
            jnp.dot(routed_in, weight[expert], preferred_element_type=F32)
            + jnp.dot(
                low_own[expert, which], right_full[expert, which], preferred_element_type=F32
            )
            for which, weight in enumerate((gate_weight, up_weight))
        ]
        if paired:
            half_rows = total_rows // 2
            sent = jnp.concatenate([value[half_rows:].astype(BF16) for value in partial], axis=1)
            got = lax.ppermute(sent, "tensor", exchange).astype(F32)
            gate = partial[0][:half_rows] + got[:, :ffw]
            up = partial[1][:half_rows] + got[:, ffw:]
            hidden = (jax.nn.silu(gate) * up).astype(BF16)
            hidden = jnp.concatenate(
                (hidden, lax.ppermute(hidden, "tensor", exchange)), axis=0
            )
        else:
            summed = lax.psum_scatter(
                jnp.concatenate(partial, axis=1), "tensor", scatter_dimension=0, tiled=True
            )
            hidden = (jax.nn.silu(summed[:, :ffw]) * summed[:, ffw:]).astype(BF16)
            hidden = lax.all_gather(hidden, "tensor", axis=0, tiled=True)
        answered = jnp.dot(hidden, down_weight[expert], preferred_element_type=F32).astype(BF16)
        mixture = mixture + route_here[:, expert : expert + 1] * answered.astype(F32)

    returned = turned(mixture.astype(BF16).reshape(shard_count, batch, part_cols))
    returned = lax.all_to_all(returned, "expert", split_axis=0, concat_axis=0, tiled=True)
    outputs = (middle_wide + jnp.sum(returned.astype(F32), axis=0)).astype(BF16)
    return outputs.reshape(steps, rows_here, part_cols)


def solution(mesh):
    return jax.shard_map(
        shards,
        mesh=mesh,
        in_specs=(
            P(None, ("groups", "expert", "dp"), None),
            P(),
            P("tensor", None),
            P(None, "tensor"),
            P(("groups", "expert", "dp"), "tensor", None),
            P(("groups", "expert", "dp")),
            P(),
            P(),
            P(None, ("groups", "expert", "dp"), None),
            P("expert", "tensor", None),
            P("expert", "tensor", None),
            P("expert", None, "tensor"),
            P(("groups", "expert"), None, "tensor", None),
            P(("groups", "expert"), None, None, "dp"),
            P("groups"),
        ),
        out_specs=P(None, ("groups", "expert", "dp"), "tensor"),
        check_vma=False,
    )
```

```python
import jax
import jax.numpy as jnp
from jax import lax
from jax.experimental import pallas as pl
from jax.experimental.pallas import tpu as pltpu
from jax.sharding import PartitionSpec as P

EPS = 1e-06
ROUTE_SCALE = 2.5
FLOOR = -1e30
F32 = jnp.float32
BF16 = jnp.bfloat16


def split_terms(value, count):
    terms = []
    for _ in range(count):
        term = lax.reduce_precision(value, 8, 7)
        terms.append(term.astype(BF16))
        value = value - term
    return terms


def exchange(items, collective_id):
    sizes = [[lax.axis_size(axis) for axis in axes] for _, axes, _ in items]
    counts = []
    for dims in sizes:
        count = 1
        for dim in dims:
            count *= dim
        counts.append(count)
    greeted = max(range(len(items)), key=lambda i: counts[i])

    def kernel(*refs):
        number = len(items)
        sources, targets = refs[:number], refs[number : 2 * number]
        sends, receives = refs[2 * number : 3 * number], refs[3 * number : 4 * number]

        def own(which):
            place = 0
            for axis, dim in zip(items[which][1], sizes[which]):
                place = place * dim + lax.axis_index(axis)
            return place

        def device(which, place):
            found = {}
            for axis, dim in reversed(list(zip(items[which][1], sizes[which]))):
                found[axis] = lax.rem(place, dim)
                place = place // dim
            return found

        barrier = pltpu.get_barrier_semaphore()
        me = own(greeted)
        for offset in range(1, counts[greeted]):
            pl.semaphore_signal(
                barrier,
                inc=1,
                device_id=device(greeted, lax.rem(me + offset, counts[greeted])),
                device_id_type=pl.DeviceIdType.MESH,
            )
        pl.semaphore_wait(barrier, counts[greeted] - 1)
        copies = []
        for which in range(number):
            me, count = own(which), counts[which]
            for offset in range(1, count):
                peer = lax.rem(me + offset, count)
                source = sources[which]
                if items[which][2] == "scatter":
                    source = source.at[peer]
                copy = pltpu.make_async_remote_copy(
                    src_ref=source,
                    dst_ref=targets[which].at[me],
                    send_sem=sends[which].at[offset - 1],
                    recv_sem=receives[which].at[offset - 1],
                    device_id=device(which, peer),
                    device_id_type=pl.DeviceIdType.MESH,
                )
                copy.start()
                copies.append(copy)
        for which in range(number):
            me = own(which)
            if items[which][2] == "scatter":
                targets[which][me] = sources[which][me]
            else:
                targets[which][me] = sources[which][...]
        for copy in copies:
            copy.wait()

    shapes = [
        array.shape if kind == "scatter" else (count, *array.shape)
        for (array, _, kind), count in zip(items, counts)
    ]
    semaphores = [pltpu.SemaphoreType.DMA((max(1, count - 1),)) for count in counts]
    return pl.pallas_call(
        kernel,
        out_shape=[
            jax.ShapeDtypeStruct(shape, array.dtype) for shape, (array, _, _) in zip(shapes, items)
        ],
        in_specs=[pl.BlockSpec(memory_space=pltpu.VMEM)] * len(items),
        out_specs=[pl.BlockSpec(memory_space=pltpu.VMEM)] * len(items),
        scratch_shapes=semaphores + semaphores,
        compiler_params=pltpu.CompilerParams(
            collective_id=collective_id, has_side_effects=True, vmem_limit_bytes=16 << 20
        ),
    )(*[array for array, _, _ in items])


def shards(
    inputs,
    attn_gain,
    qkv_weight,
    out_weight,
    cache,
    lengths,
    moe_gain,
    router_weight,
    expert_ids,
    gate_weight,
    up_weight,
    down_weight,
    pool_left,
    pool_right,
    pair_slot,
):
    steps, rows_here, width = inputs.shape
    experts_here, part_cols, ffw = gate_weight.shape
    slots_here, _, _, rank = pool_left.shape
    right_cols = pool_right.shape[3]
    lat = cache.shape[2]
    span_here = cache.shape[1]
    shard_count = lax.axis_size("expert")
    shard_index = lax.axis_index("expert")
    tensor_count = lax.axis_size("tensor")
    tensor_index = lax.axis_index("tensor")
    expert_count = shard_count * experts_here
    col_start = tensor_index * part_cols
    batch = steps * rows_here
    total_rows = shard_count * batch
    score_scale = lat ** (-0.5)
    paired = tensor_count == 2

    own_slots = shard_index * slots_here + jnp.arange(slots_here, dtype=jnp.int32)
    serves = (pair_slot[:, None] == own_slots[None, :]).astype(BF16)

    piece_cols = right_cols // tensor_count
    right_piece = lax.dynamic_slice_in_dim(pool_right, tensor_index * piece_cols, piece_cols, 3)
    right_sent = jnp.einsum(
        "es,sxrf->exrf", serves, right_piece, preferred_element_type=F32
    ).astype(BF16)
    right_sent = right_sent.reshape(shard_count, experts_here, 2, rank, piece_cols)
    right_got = lax.all_to_all(right_sent, "expert", split_axis=0, concat_axis=0, tiled=True)
    right_own = jnp.sum(right_got.astype(F32), axis=0).astype(BF16)
    right_full = lax.all_gather(right_own, ("dp", "tensor"), axis=3, tiled=True)

    chosen = jnp.any(
        expert_ids.reshape(batch, -1)[:, :, None]
        == jnp.arange(expert_count, dtype=jnp.int32)[None, None, :],
        axis=1,
    ).astype(F32)

    tokens = inputs.reshape(batch, width)
    tokens_wide = tokens.astype(F32)
    square_mean = jnp.mean(tokens_wide * tokens_wide, axis=-1, keepdims=True)
    token_cols = lax.dynamic_slice_in_dim(tokens, col_start, part_cols, 1)
    gain_piece = lax.dynamic_slice_in_dim(attn_gain, col_start, part_cols, 0)
    normed_cols = (
        token_cols.astype(F32) * lax.rsqrt(square_mean + EPS) * gain_piece
    ).astype(BF16)
    projected = jnp.dot(normed_cols, qkv_weight, preferred_element_type=F32)
    projected = jnp.sum(exchange([(projected, ("tensor",), "gather")], 0)[0], axis=0)
    queries = projected[:, :lat].astype(BF16).reshape(steps, rows_here, lat)
    fresh = projected[:, lat:].astype(BF16).reshape(steps, rows_here, lat)

    positions = tensor_index * span_here + jnp.arange(span_here, dtype=jnp.int32)
    visible = (positions[None, :] < lengths[:, None])[:, None, :]
    scores = (
        jnp.einsum("sbl,bpl->bsp", queries, cache, preferred_element_type=F32) * score_scale
    )
    local_top = jnp.max(jnp.where(visible, scores, FLOOR), axis=-1, keepdims=True)
    weights = jnp.where(visible, jnp.exp(scores - local_top), 0.0)
    terms = jnp.concatenate(split_terms(weights, 3), axis=1)
    sums = jnp.einsum("bmp,bpl->bml", terms, cache, preferred_element_type=F32)
    sums = jnp.sum(sums.reshape(rows_here, 3, steps, lat), axis=1)
    local_total = jnp.sum(weights, axis=-1, keepdims=True)
    packed = jnp.concatenate(
        (
            sums,
            jnp.broadcast_to(local_top, (rows_here, steps, 64)),
            jnp.broadcast_to(local_total, (rows_here, steps, 64)),
        ),
        axis=2,
    )
    packed = packed.reshape(rows_here * steps, lat + 128)
    parts = exchange([(packed, ("tensor",), "gather")], 1)[0]
    parts = parts.reshape(tensor_count, rows_here, steps, lat + 128)
    part_sums, part_tops, part_totals = (
        parts[..., :lat],
        parts[..., lat],
        parts[..., lat + 64],
    )

    fresh_wide = fresh.astype(F32)
    latest = (
        jnp.sum(queries.astype(F32)[:, None] * fresh_wide[None], axis=-1) * score_scale
    )
    step_range = jnp.arange(steps)
    usable = (step_range[None, :] <= step_range[:, None])[:, :, None]
    latest_top = jnp.max(jnp.where(usable, latest, FLOOR), axis=1)
    highest = jnp.maximum(jnp.max(part_tops, axis=0), latest_top.T)
    factors = jnp.exp(part_tops - highest[None])
    latest_weights = jnp.where(usable, jnp.exp(latest - highest.T[:, None, :]), 0.0)
    denominator = jnp.sum(part_totals * factors, axis=0) + jnp.sum(latest_weights, axis=1).T
    numerator = jnp.sum(part_sums * factors[..., None], axis=0).transpose(1, 0, 2) + jnp.sum(
        latest_weights[..., None] * fresh_wide[None], axis=1
    )
    attended = (numerator / denominator.T[..., None]).astype(BF16).reshape(batch, lat)
    middle = (
        token_cols.astype(F32) + jnp.dot(attended, out_weight, preferred_element_type=F32)
    ).astype(BF16)

    gain_cols = lax.dynamic_slice_in_dim(moe_gain, col_start, part_cols, 0)
    router_rows = lax.dynamic_slice_in_dim(router_weight, col_start, part_cols, 0).astype(F32)
    middle_wide = middle.astype(F32)
    partial_logits = jnp.dot(
        middle_wide * gain_cols, router_rows, precision=lax.Precision.HIGHEST
    )
    partial_squares = jnp.sum(middle_wide * middle_wide, axis=-1, keepdims=True)
    statistics = jnp.concatenate(
        (
            partial_logits,
            jnp.where(tensor_index == 0, chosen, 0.0),
            jnp.broadcast_to(partial_squares, (batch, 128 - 2 * expert_count)),
        ),
        axis=1,
    )
    statistics, middle_all = exchange(
        [(statistics, ("expert", "tensor"), "gather"), (middle, ("expert",), "gather")], 2
    )
    statistics = jnp.sum(
        statistics.reshape(shard_count, tensor_count, batch, 128), axis=1
    )

    def turned(value):
        if not paired:
            return value
        half = shard_count // 2
        swapped = jnp.concatenate((value[half:], value[:half]), axis=0)
        return jnp.where(tensor_index == 0, value, swapped)

    statistics = turned(statistics).reshape(total_rows, 128)
    rows_all = turned(middle_all).reshape(total_rows, part_cols)
    mask_all = statistics[:, expert_count : 2 * expert_count]

    inverse = lax.rsqrt(statistics[:, 127:] / width + EPS)
    routed_in = (rows_all.astype(F32) * inverse * gain_cols).astype(BF16)
    gated = jax.nn.sigmoid(inverse * statistics[:, :expert_count]) * mask_all
    route = (ROUTE_SCALE * gated / jnp.sum(gated, axis=-1, keepdims=True)).astype(BF16)
    route_here = lax.dynamic_slice_in_dim(
        route, shard_index * experts_here, experts_here, 1
    ).astype(F32)

    low = jnp.einsum("nd,sxdr->snxr", routed_in, pool_left, preferred_element_type=F32)
    low = low.astype(BF16).reshape(slots_here, total_rows, 2 * rank)
    low_sent = jnp.einsum("es,snq->enq", serves, low, preferred_element_type=F32).astype(BF16)
    low_sent = low_sent.reshape(shard_count, experts_here * total_rows, 2 * rank)
    low_got = exchange([(low_sent, ("expert",), "scatter")], 3)[0]
    low_own = jnp.sum(low_got.astype(F32), axis=0).astype(BF16)
    low_own = low_own.reshape(experts_here, total_rows, 2, rank)

    swap = [(0, 1), (1, 0)]
    mixture = jnp.zeros((total_rows, part_cols), F32)
    for expert in range(experts_here):
        partial = [
            jnp.dot(routed_in, weight[expert], preferred_element_type=F32)
            + jnp.dot(
                low_own[expert, :, which], right_full[expert, which], preferred_element_type=F32
            )
            for which, weight in enumerate((gate_weight, up_weight))
        ]
        if paired:
            half_rows = total_rows // 2
            sent = jnp.concatenate([value[half_rows:].astype(BF16) for value in partial], axis=1)
            got = lax.ppermute(sent, "tensor", swap).astype(F32)
            gate = partial[0][:half_rows] + got[:, :ffw]
            up = partial[1][:half_rows] + got[:, ffw:]
            hidden = (jax.nn.silu(gate) * up).astype(BF16)
            hidden = jnp.concatenate(
                (hidden, lax.ppermute(hidden, "tensor", swap)), axis=0
            )
        else:
            summed = lax.psum_scatter(
                jnp.concatenate(partial, axis=1), "tensor", scatter_dimension=0, tiled=True
            )
            hidden = (jax.nn.silu(summed[:, :ffw]) * summed[:, ffw:]).astype(BF16)
            hidden = lax.all_gather(hidden, "tensor", axis=0, tiled=True)
        answered = jnp.dot(hidden, down_weight[expert], preferred_element_type=F32).astype(BF16)
        mixture = mixture + route_here[:, expert : expert + 1] * answered.astype(F32)

    returned = turned(mixture.astype(BF16).reshape(shard_count, batch, part_cols))
    returned = exchange([(returned, ("expert",), "scatter")], 4)[0]
    outputs = (middle_wide + jnp.sum(returned.astype(F32), axis=0)).astype(BF16)
    return outputs.reshape(steps, rows_here, part_cols)


def solution(mesh):
    return jax.shard_map(
        shards,
        mesh=mesh,
        in_specs=(
            P(None, ("groups", "expert", "dp"), None),
            P(),
            P("tensor", None),
            P(None, "tensor"),
            P(("groups", "expert", "dp"), "tensor", None),
            P(("groups", "expert", "dp")),
            P(),
            P(),
            P(None, ("groups", "expert", "dp"), None),
            P("expert", "tensor", None),
            P("expert", "tensor", None),
            P("expert", None, "tensor"),
            P(("groups", "expert"), None, "tensor", None),
            P(("groups", "expert"), None, None, "dp"),
            P("groups"),
        ),
        out_specs=P(None, ("groups", "expert", "dp"), "tensor"),
        check_vma=False,
    )
```

```python
import jax
import jax.numpy as jnp
from jax import lax
from jax.experimental import pallas as pl
from jax.experimental.pallas import tpu as pltpu
from jax.sharding import PartitionSpec as P

EPS = 1e-06
ROUTE_SCALE = 2.5
FLOOR = -1e30
F32 = jnp.float32
BF16 = jnp.bfloat16


def split_terms(value, count):
    terms = []
    for _ in range(count):
        term = lax.reduce_precision(value, 8, 7)
        terms.append(term.astype(BF16))
        value = value - term
    return terms


def exchange(items, collective_id):
    sizes = [[lax.axis_size(axis) for axis in axes] for _, axes, _ in items]
    counts = []
    for dims in sizes:
        count = 1
        for dim in dims:
            count *= dim
        counts.append(count)
    greeted = max(range(len(items)), key=lambda i: counts[i])

    def kernel(*refs):
        number = len(items)
        sources, targets = refs[:number], refs[number : 2 * number]
        sends, receives = refs[2 * number : 3 * number], refs[3 * number : 4 * number]

        def own(which):
            place = 0
            for axis, dim in zip(items[which][1], sizes[which]):
                place = place * dim + lax.axis_index(axis)
            return place

        def device(which, place):
            found = {}
            for axis, dim in reversed(list(zip(items[which][1], sizes[which]))):
                found[axis] = lax.rem(place, dim)
                place = place // dim
            return found

        barrier = pltpu.get_barrier_semaphore()
        me = own(greeted)
        for offset in range(1, counts[greeted]):
            pl.semaphore_signal(
                barrier,
                inc=1,
                device_id=device(greeted, lax.rem(me + offset, counts[greeted])),
                device_id_type=pl.DeviceIdType.MESH,
            )
        pl.semaphore_wait(barrier, counts[greeted] - 1)
        copies = []
        for which in range(number):
            me, count = own(which), counts[which]
            for offset in range(1, count):
                peer = lax.rem(me + offset, count)
                source = sources[which]
                if items[which][2] == "scatter":
                    source = source.at[peer]
                copy = pltpu.make_async_remote_copy(
                    src_ref=source,
                    dst_ref=targets[which].at[me],
                    send_sem=sends[which].at[offset - 1],
                    recv_sem=receives[which].at[offset - 1],
                    device_id=device(which, peer),
                    device_id_type=pl.DeviceIdType.MESH,
                )
                copy.start()
                copies.append(copy)
        for which in range(number):
            me = own(which)
            if items[which][2] == "scatter":
                targets[which][me] = sources[which][me]
            else:
                targets[which][me] = sources[which][...]
        for copy in copies:
            copy.wait()

    shapes = [
        array.shape if kind == "scatter" else (count, *array.shape)
        for (array, _, kind), count in zip(items, counts)
    ]
    semaphores = [pltpu.SemaphoreType.DMA((max(1, count - 1),)) for count in counts]
    return pl.pallas_call(
        kernel,
        out_shape=[
            jax.ShapeDtypeStruct(shape, array.dtype) for shape, (array, _, _) in zip(shapes, items)
        ],
        in_specs=[pl.BlockSpec(memory_space=pltpu.VMEM)] * len(items),
        out_specs=[pl.BlockSpec(memory_space=pltpu.VMEM)] * len(items),
        scratch_shapes=semaphores + semaphores,
        compiler_params=pltpu.CompilerParams(
            collective_id=collective_id, has_side_effects=True, vmem_limit_bytes=16 << 20
        ),
    )(*[array for array, _, _ in items])


def expert_stage(rows, low_sent, right, route, gate, up, down):
    count, depth, ffw = gate.shape
    total = rows.shape[0]
    half = total // 2
    cols = down.shape[2]
    rank = right.shape[2]
    sources = low_sent.shape[0]
    block = total // sources
    tile = 256 if cols % 256 == 0 and ffw % 256 == 0 else 128
    mesh_ids = pl.DeviceIdType.MESH

    def kernel(
        rows_ref, low_ref, right_ref, route_ref, gate_ref, up_ref, down_ref, back_ref,
        low_got, in_weights, out_weights, whole, own, sent, got, hidden, mixture, mixed,
        in_sem, out_sem, low_send, low_recv, pre_send, pre_recv, hid_send, hid_recv,
        back_send, back_recv,
    ):
        me = lax.axis_index("expert")
        side = lax.axis_index("tensor")
        other = {"tensor": 1 - side}
        peers = [lax.rem(me + offset, sources) for offset in range(1, sources)]

        def load_in(e):
            return [
                pltpu.make_async_copy(
                    ref.at[e], in_weights.at[e % 2, which], in_sem.at[e % 2, which]
                )
                for which, ref in enumerate((gate_ref, up_ref))
            ]

        def load_out(e):
            return pltpu.make_async_copy(down_ref.at[e], out_weights.at[e % 2], out_sem.at[e % 2])

        for e in range(min(2, count)):
            for copy in load_in(e):
                copy.start()
        for e in range(min(2, count)):
            load_out(e).start()

        barrier = pltpu.get_barrier_semaphore()
        for target in [other] + [{"expert": peer} for peer in peers]:
            pl.semaphore_signal(barrier, inc=1, device_id=target, device_id_type=mesh_ids)
        pl.semaphore_wait(barrier, sources)

        low_copies = []
        for at, peer in enumerate(peers):
            copy = pltpu.make_async_remote_copy(
                src_ref=low_ref.at[peer],
                dst_ref=low_got.at[me],
                send_sem=low_send.at[at],
                recv_sem=low_recv.at[at],
                device_id={"expert": peer},
                device_id_type=mesh_ids,
            )
            copy.start()
            low_copies.append(copy)
        low_got[me] = low_ref[me]
        mixture[...] = jnp.zeros_like(mixture)

        pre_copies = [
            pltpu.make_async_remote_copy(
                src_ref=sent.at[e],
                dst_ref=got.at[e],
                send_sem=pre_send.at[e],
                recv_sem=pre_recv.at[e],
                device_id=other,
                device_id_type=mesh_ids,
            )
            for e in range(count)
        ]
        hid_copies = [
            pltpu.make_async_remote_copy(
                src_ref=hidden.at[e, pl.ds(0, half)],
                dst_ref=hidden.at[e, pl.ds(half, half)],
                send_sem=hid_send.at[e],
                recv_sem=hid_recv.at[e],
                device_id=other,
                device_id_type=mesh_ids,
            )
            for e in range(count)
        ]

        def project(e):
            for copy in load_in(e):
                copy.wait()
            for which in range(2):

                @pl.loop(0, ffw // tile)
                def _(step):
                    start = pl.multiple_of(step * tile, tile)
                    whole[which, :, pl.ds(start, tile)] = jnp.dot(
                        rows_ref[...],
                        in_weights[e % 2, which, :, pl.ds(start, tile)],
                        preferred_element_type=F32,
                    )

            if e + 2 < count:
                for copy in load_in(e + 2):
                    copy.start()
            if e == 0:
                for copy in low_copies:
                    copy.wait()
            low = low_got[0, pl.ds(e * total, total)].astype(F32)
            for source in range(1, sources):
                low = low + low_got[source, pl.ds(e * total, total)].astype(F32)
            low = low.astype(BF16)
            for which in range(2):
                value = whole[which] + jnp.dot(
                    low[:, which * rank : (which + 1) * rank],
                    right_ref[e, which],
                    preferred_element_type=F32,
                )
                own[e % 2, which] = value[:half]
                sent[e, which] = value[half:].astype(BF16)
            pre_copies[e].start()

        def activate(e):
            pre_copies[e].wait_recv()
            gate_sum = own[e % 2, 0] + got[e, 0].astype(F32)
            up_sum = own[e % 2, 1] + got[e, 1].astype(F32)
            value = gate_sum / (1.0 + jnp.exp(-gate_sum)) * up_sum
            hidden[e, pl.ds(0, half)] = value.astype(BF16)
            hid_copies[e].start()

        def answer(e):
            load_out(e).wait()
            hid_copies[e].wait_recv()

            @pl.loop(0, cols // tile)
            def _(step):
                start = pl.multiple_of(step * tile, tile)
                value = jnp.dot(
                    hidden[e],
                    out_weights[e % 2, :, pl.ds(start, tile)],
                    preferred_element_type=F32,
                )
                mixture[:, pl.ds(start, tile)] += route_ref[:, e : e + 1] * value.astype(
                    BF16
                ).astype(F32)

            if e + 2 < count:
                load_out(e + 2).start()

        for e in range(count):
            project(e)
            if e >= 1:
                activate(e - 1)
            if e >= 2:
                answer(e - 2)
        activate(count - 1)
        if count >= 2:
            answer(count - 2)
        answer(count - 1)

        for place in range(sources):
            mixed[place] = mixture[pl.ds(place * block, block)].astype(BF16)
        turn = side * (sources // 2)
        back_copies = []
        for at, peer in enumerate(peers):
            copy = pltpu.make_async_remote_copy(
                src_ref=mixed.at[lax.rem(peer + turn, sources)],
                dst_ref=back_ref.at[me],
                send_sem=back_send.at[at],
                recv_sem=back_recv.at[at],
                device_id={"expert": peer},
                device_id_type=mesh_ids,
            )
            copy.start()
            back_copies.append(copy)
        back_ref[me] = mixed[lax.rem(me + turn, sources)]
        for e in range(count):
            pre_copies[e].wait_send()
            hid_copies[e].wait_send()
        for copy in back_copies:
            copy.wait()

    semaphores = pltpu.SemaphoreType.DMA
    in_vmem = pl.BlockSpec(memory_space=pltpu.VMEM)
    in_place = pl.BlockSpec(memory_space=pl.ANY)
    return pl.pallas_call(
        kernel,
        out_shape=jax.ShapeDtypeStruct((sources, block, cols), BF16),
        in_specs=[in_vmem] * 4 + [in_place] * 3,
        out_specs=in_vmem,
        scratch_shapes=[
            pltpu.VMEM(low_sent.shape, BF16),
            pltpu.VMEM((2, 2, depth, ffw), BF16),
            pltpu.VMEM((2, ffw, cols), BF16),
            pltpu.VMEM((2, total, ffw), F32),
            pltpu.VMEM((2, 2, half, ffw), F32),
            pltpu.VMEM((count, 2, half, ffw), BF16),
            pltpu.VMEM((count, 2, half, ffw), BF16),
            pltpu.VMEM((count, total, ffw), BF16),
            pltpu.VMEM((total, cols), F32),
            pltpu.VMEM((sources, block, cols), BF16),
            semaphores((2, 2)),
            semaphores((2,)),
            semaphores((sources - 1,)),
            semaphores((sources - 1,)),
            semaphores((count,)),
            semaphores((count,)),
            semaphores((count,)),
            semaphores((count,)),
            semaphores((sources - 1,)),
            semaphores((sources - 1,)),
        ],
        compiler_params=pltpu.CompilerParams(
            collective_id=5, has_side_effects=True, vmem_limit_bytes=44 << 20
        ),
    )(rows, low_sent, right, route, gate, up, down)


def shards(
    inputs,
    attn_gain,
    qkv_weight,
    out_weight,
    cache,
    lengths,
    moe_gain,
    router_weight,
    expert_ids,
    gate_weight,
    up_weight,
    down_weight,
    pool_left,
    pool_right,
    pair_slot,
):
    steps, rows_here, width = inputs.shape
    experts_here, part_cols, ffw = gate_weight.shape
    slots_here, _, _, rank = pool_left.shape
    right_cols = pool_right.shape[3]
    lat = cache.shape[2]
    span_here = cache.shape[1]
    shard_count = lax.axis_size("expert")
    shard_index = lax.axis_index("expert")
    tensor_count = lax.axis_size("tensor")
    tensor_index = lax.axis_index("tensor")
    expert_count = shard_count * experts_here
    col_start = tensor_index * part_cols
    batch = steps * rows_here
    total_rows = shard_count * batch
    score_scale = lat ** (-0.5)
    paired = tensor_count == 2

    own_slots = shard_index * slots_here + jnp.arange(slots_here, dtype=jnp.int32)
    serves = (pair_slot[:, None] == own_slots[None, :]).astype(BF16)

    piece_cols = right_cols // tensor_count
    right_piece = lax.dynamic_slice_in_dim(pool_right, tensor_index * piece_cols, piece_cols, 3)
    right_sent = jnp.einsum(
        "es,sxrf->exrf", serves, right_piece, preferred_element_type=F32
    ).astype(BF16)
    right_sent = right_sent.reshape(shard_count, experts_here, 2, rank, piece_cols)
    right_got = lax.all_to_all(right_sent, "expert", split_axis=0, concat_axis=0, tiled=True)
    right_own = jnp.sum(right_got.astype(F32), axis=0).astype(BF16)
    right_full = lax.all_gather(right_own, ("dp", "tensor"), axis=3, tiled=True)

    chosen = jnp.any(
        expert_ids.reshape(batch, -1)[:, :, None]
        == jnp.arange(expert_count, dtype=jnp.int32)[None, None, :],
        axis=1,
    ).astype(F32)

    tokens = inputs.reshape(batch, width)
    tokens_wide = tokens.astype(F32)
    square_mean = jnp.mean(tokens_wide * tokens_wide, axis=-1, keepdims=True)
    token_cols = lax.dynamic_slice_in_dim(tokens, col_start, part_cols, 1)
    gain_piece = lax.dynamic_slice_in_dim(attn_gain, col_start, part_cols, 0)
    normed_cols = (
        token_cols.astype(F32) * lax.rsqrt(square_mean + EPS) * gain_piece
    ).astype(BF16)
    projected = jnp.dot(normed_cols, qkv_weight, preferred_element_type=F32)
    projected = jnp.sum(exchange([(projected, ("tensor",), "gather")], 0)[0], axis=0)
    queries = projected[:, :lat].astype(BF16).reshape(steps, rows_here, lat)
    fresh = projected[:, lat:].astype(BF16).reshape(steps, rows_here, lat)

    positions = tensor_index * span_here + jnp.arange(span_here, dtype=jnp.int32)
    visible = (positions[None, :] < lengths[:, None])[:, None, :]
    scores = (
        jnp.einsum("sbl,bpl->bsp", queries, cache, preferred_element_type=F32) * score_scale
    )
    local_top = jnp.max(jnp.where(visible, scores, FLOOR), axis=-1, keepdims=True)
    weights = jnp.where(visible, jnp.exp(scores - local_top), 0.0)
    terms = jnp.concatenate(split_terms(weights, 3), axis=1)
    sums = jnp.einsum("bmp,bpl->bml", terms, cache, preferred_element_type=F32)
    sums = jnp.sum(sums.reshape(rows_here, 3, steps, lat), axis=1)
    local_total = jnp.sum(weights, axis=-1, keepdims=True)
    packed = jnp.concatenate(
        (
            sums,
            jnp.broadcast_to(local_top, (rows_here, steps, 64)),
            jnp.broadcast_to(local_total, (rows_here, steps, 64)),
        ),
        axis=2,
    )
    packed = packed.reshape(rows_here * steps, lat + 128)
    parts = exchange([(packed, ("tensor",), "gather")], 1)[0]
    parts = parts.reshape(tensor_count, rows_here, steps, lat + 128)
    part_sums, part_tops, part_totals = (
        parts[..., :lat],
        parts[..., lat],
        parts[..., lat + 64],
    )

    fresh_wide = fresh.astype(F32)
    latest = (
        jnp.sum(queries.astype(F32)[:, None] * fresh_wide[None], axis=-1) * score_scale
    )
    step_range = jnp.arange(steps)
    usable = (step_range[None, :] <= step_range[:, None])[:, :, None]
    latest_top = jnp.max(jnp.where(usable, latest, FLOOR), axis=1)
    highest = jnp.maximum(jnp.max(part_tops, axis=0), latest_top.T)
    factors = jnp.exp(part_tops - highest[None])
    latest_weights = jnp.where(usable, jnp.exp(latest - highest.T[:, None, :]), 0.0)
    denominator = jnp.sum(part_totals * factors, axis=0) + jnp.sum(latest_weights, axis=1).T
    numerator = jnp.sum(part_sums * factors[..., None], axis=0).transpose(1, 0, 2) + jnp.sum(
        latest_weights[..., None] * fresh_wide[None], axis=1
    )
    attended = (numerator / denominator.T[..., None]).astype(BF16).reshape(batch, lat)
    middle = (
        token_cols.astype(F32) + jnp.dot(attended, out_weight, preferred_element_type=F32)
    ).astype(BF16)

    gain_cols = lax.dynamic_slice_in_dim(moe_gain, col_start, part_cols, 0)
    router_rows = lax.dynamic_slice_in_dim(router_weight, col_start, part_cols, 0).astype(F32)
    middle_wide = middle.astype(F32)
    partial_logits = jnp.dot(
        middle_wide * gain_cols, router_rows, precision=lax.Precision.HIGHEST
    )
    partial_squares = jnp.sum(middle_wide * middle_wide, axis=-1, keepdims=True)
    statistics = jnp.concatenate(
        (
            partial_logits,
            jnp.where(tensor_index == 0, chosen, 0.0),
            jnp.broadcast_to(partial_squares, (batch, 128 - 2 * expert_count)),
        ),
        axis=1,
    )
    statistics, middle_all = exchange(
        [(statistics, ("expert", "tensor"), "gather"), (middle, ("expert",), "gather")], 2
    )
    statistics = jnp.sum(
        statistics.reshape(shard_count, tensor_count, batch, 128), axis=1
    )

    def turned(value):
        if not paired:
            return value
        half = shard_count // 2
        swapped = jnp.concatenate((value[half:], value[:half]), axis=0)
        return jnp.where(tensor_index == 0, value, swapped)

    statistics = turned(statistics).reshape(total_rows, 128)
    rows_all = turned(middle_all).reshape(total_rows, part_cols)
    mask_all = statistics[:, expert_count : 2 * expert_count]

    inverse = lax.rsqrt(statistics[:, 127:] / width + EPS)
    routed_in = (rows_all.astype(F32) * inverse * gain_cols).astype(BF16)
    gated = jax.nn.sigmoid(inverse * statistics[:, :expert_count]) * mask_all
    route = (ROUTE_SCALE * gated / jnp.sum(gated, axis=-1, keepdims=True)).astype(BF16)
    route_here = lax.dynamic_slice_in_dim(
        route, shard_index * experts_here, experts_here, 1
    ).astype(F32)

    low = jnp.einsum("nd,sxdr->snxr", routed_in, pool_left, preferred_element_type=F32)
    low = low.astype(BF16).reshape(slots_here, total_rows, 2 * rank)
    low_sent = jnp.einsum("es,snq->enq", serves, low, preferred_element_type=F32).astype(BF16)
    low_sent = low_sent.reshape(shard_count, experts_here * total_rows, 2 * rank)
    if paired:
        returned = expert_stage(
            routed_in, low_sent, right_full, route_here, gate_weight, up_weight, down_weight
        )
    else:
        low_got = exchange([(low_sent, ("expert",), "scatter")], 3)[0]
        low_own = jnp.sum(low_got.astype(F32), axis=0).astype(BF16)
        low_own = low_own.reshape(experts_here, total_rows, 2, rank)
        mixture = jnp.zeros((total_rows, part_cols), F32)
        for expert in range(experts_here):
            partial = [
                jnp.dot(routed_in, weight[expert], preferred_element_type=F32)
                + jnp.dot(
                    low_own[expert, :, which],
                    right_full[expert, which],
                    preferred_element_type=F32,
                )
                for which, weight in enumerate((gate_weight, up_weight))
            ]
            summed = lax.psum_scatter(
                jnp.concatenate(partial, axis=1), "tensor", scatter_dimension=0, tiled=True
            )
            hidden = (jax.nn.silu(summed[:, :ffw]) * summed[:, ffw:]).astype(BF16)
            hidden = lax.all_gather(hidden, "tensor", axis=0, tiled=True)
            answered = jnp.dot(hidden, down_weight[expert], preferred_element_type=F32)
            weight = route_here[:, expert : expert + 1]
            mixture = mixture + weight * answered.astype(BF16).astype(F32)
        returned = mixture.astype(BF16).reshape(shard_count, batch, part_cols)
        returned = exchange([(returned, ("expert",), "scatter")], 4)[0]
    outputs = (middle_wide + jnp.sum(returned.astype(F32), axis=0)).astype(BF16)
    return outputs.reshape(steps, rows_here, part_cols)


def solution(mesh):
    return jax.shard_map(
        shards,
        mesh=mesh,
        in_specs=(
            P(None, ("groups", "expert", "dp"), None),
            P(),
            P("tensor", None),
            P(None, "tensor"),
            P(("groups", "expert", "dp"), "tensor", None),
            P(("groups", "expert", "dp")),
            P(),
            P(),
            P(None, ("groups", "expert", "dp"), None),
            P("expert", "tensor", None),
            P("expert", "tensor", None),
            P("expert", None, "tensor"),
            P(("groups", "expert"), None, "tensor", None),
            P(("groups", "expert"), None, None, "dp"),
            P("groups"),
        ),
        out_specs=P(None, ("groups", "expert", "dp"), "tensor"),
        check_vma=False,
    )
```

```python
import jax
import jax.numpy as jnp
from jax import lax
from jax.experimental import pallas as pl
from jax.experimental.pallas import tpu as pltpu
from jax.sharding import PartitionSpec as P

EPS = 1e-06
ROUTE_SCALE = 2.5
FLOOR = -1e30
F32 = jnp.float32
BF16 = jnp.bfloat16


def split_terms(value, count):
    terms = []
    for _ in range(count):
        term = lax.reduce_precision(value, 8, 7)
        terms.append(term.astype(BF16))
        value = value - term
    return terms


def exchange(items, collective_id, group=None):
    sizes = [[lax.axis_size(axis) for axis in axes] for _, axes, _ in items]
    counts = []
    for dims in sizes:
        count = 1
        for dim in dims:
            count *= dim
        counts.append(count)
    greeted = group or items[max(range(len(items)), key=lambda i: counts[i])][1]
    greeted_sizes = [lax.axis_size(axis) for axis in greeted]
    greeted_count = 1
    for dim in greeted_sizes:
        greeted_count *= dim

    def kernel(*refs):
        number = len(items)
        sources, targets = refs[:number], refs[number : 2 * number]
        sends, receives = refs[2 * number : 3 * number], refs[3 * number : 4 * number]

        def own(axes, dims):
            place = 0
            for axis, dim in zip(axes, dims):
                place = place * dim + lax.axis_index(axis)
            return place

        def device(axes, dims, place):
            found = {}
            for axis, dim in reversed(list(zip(axes, dims))):
                found[axis] = lax.rem(place, dim)
                place = place // dim
            return found

        barrier = pltpu.get_barrier_semaphore()
        me = own(greeted, greeted_sizes)
        for offset in range(1, greeted_count):
            pl.semaphore_signal(
                barrier,
                inc=1,
                device_id=device(greeted, greeted_sizes, lax.rem(me + offset, greeted_count)),
                device_id_type=pl.DeviceIdType.MESH,
            )
        pl.semaphore_wait(barrier, greeted_count - 1)
        copies = []
        for which in range(number):
            me, count = own(items[which][1], sizes[which]), counts[which]
            for offset in range(1, count):
                peer = lax.rem(me + offset, count)
                source = sources[which]
                if items[which][2] == "scatter":
                    source = source.at[peer]
                copy = pltpu.make_async_remote_copy(
                    src_ref=source,
                    dst_ref=targets[which].at[me],
                    send_sem=sends[which].at[offset - 1],
                    recv_sem=receives[which].at[offset - 1],
                    device_id=device(items[which][1], sizes[which], peer),
                    device_id_type=pl.DeviceIdType.MESH,
                )
                copy.start()
                copies.append(copy)
        for which in range(number):
            me = own(items[which][1], sizes[which])
            if items[which][2] == "scatter":
                targets[which][me] = sources[which][me]
            else:
                targets[which][me] = sources[which][...]
        for copy in copies:
            copy.wait()

    shapes = [
        array.shape if kind == "scatter" else (count, *array.shape)
        for (array, _, kind), count in zip(items, counts)
    ]
    semaphores = [pltpu.SemaphoreType.DMA((max(1, count - 1),)) for count in counts]
    return pl.pallas_call(
        kernel,
        out_shape=[
            jax.ShapeDtypeStruct(shape, array.dtype) for shape, (array, _, _) in zip(shapes, items)
        ],
        in_specs=[pl.BlockSpec(memory_space=pltpu.VMEM)] * len(items),
        out_specs=[pl.BlockSpec(memory_space=pltpu.VMEM)] * len(items),
        scratch_shapes=semaphores + semaphores,
        compiler_params=pltpu.CompilerParams(
            collective_id=collective_id, has_side_effects=True, vmem_limit_bytes=16 << 20
        ),
    )(*[array for array, _, _ in items])


def expert_stage(rows, low_sent, right, route, gate, up, down):
    count, depth, ffw = gate.shape
    total = rows.shape[0]
    half = total // 2
    cols = down.shape[2]
    rank = right.shape[2]
    sources = low_sent.shape[0]
    block = total // sources
    tile = 256 if cols % 256 == 0 and ffw % 256 == 0 else 128
    mesh_ids = pl.DeviceIdType.MESH

    def kernel(
        rows_ref, low_ref, right_ref, route_ref, gate_ref, up_ref, down_ref, back_ref,
        low_got, in_weights, out_weights, whole, own, sent, got, hidden, mixture, mixed,
        in_sem, out_sem, low_send, low_recv, pre_send, pre_recv, hid_send, hid_recv,
        back_send, back_recv,
    ):
        me = lax.axis_index("expert")
        side = lax.axis_index("tensor")
        other = {"tensor": 1 - side}
        peers = [lax.rem(me + offset, sources) for offset in range(1, sources)]

        def load_in(e):
            return [
                pltpu.make_async_copy(
                    ref.at[e], in_weights.at[e % 2, which], in_sem.at[e % 2, which]
                )
                for which, ref in enumerate((gate_ref, up_ref))
            ]

        def load_out(e):
            return pltpu.make_async_copy(down_ref.at[e], out_weights.at[e % 2], out_sem.at[e % 2])

        for e in range(min(2, count)):
            for copy in load_in(e):
                copy.start()
        for e in range(min(2, count)):
            load_out(e).start()

        barrier = pltpu.get_barrier_semaphore()
        for target in [other] + [{"expert": peer} for peer in peers]:
            pl.semaphore_signal(barrier, inc=1, device_id=target, device_id_type=mesh_ids)
        pl.semaphore_wait(barrier, sources)

        low_copies = []
        for at, peer in enumerate(peers):
            copy = pltpu.make_async_remote_copy(
                src_ref=low_ref.at[peer],
                dst_ref=low_got.at[me],
                send_sem=low_send.at[at],
                recv_sem=low_recv.at[at],
                device_id={"expert": peer},
                device_id_type=mesh_ids,
            )
            copy.start()
            low_copies.append(copy)
        low_got[me] = low_ref[me]
        mixture[...] = jnp.zeros_like(mixture)

        pre_copies = [
            pltpu.make_async_remote_copy(
                src_ref=sent.at[e],
                dst_ref=got.at[e],
                send_sem=pre_send.at[e],
                recv_sem=pre_recv.at[e],
                device_id=other,
                device_id_type=mesh_ids,
            )
            for e in range(count)
        ]
        hid_copies = [
            pltpu.make_async_remote_copy(
                src_ref=hidden.at[e, pl.ds(0, half)],
                dst_ref=hidden.at[e, pl.ds(half, half)],
                send_sem=hid_send.at[e],
                recv_sem=hid_recv.at[e],
                device_id=other,
                device_id_type=mesh_ids,
            )
            for e in range(count)
        ]

        def project(e):
            for copy in load_in(e):
                copy.wait()
            for which in range(2):

                @pl.loop(0, ffw // tile)
                def _(step):
                    start = pl.multiple_of(step * tile, tile)
                    whole[which, :, pl.ds(start, tile)] = jnp.dot(
                        rows_ref[...],
                        in_weights[e % 2, which, :, pl.ds(start, tile)],
                        preferred_element_type=F32,
                    )

            if e + 2 < count:
                for copy in load_in(e + 2):
                    copy.start()
            if e == 0:
                for copy in low_copies:
                    copy.wait()
            low = low_got[0, pl.ds(e * total, total)].astype(F32)
            for source in range(1, sources):
                low = low + low_got[source, pl.ds(e * total, total)].astype(F32)
            low = low.astype(BF16)
            for which in range(2):
                value = whole[which] + jnp.dot(
                    low[:, which * rank : (which + 1) * rank],
                    right_ref[e, which],
                    preferred_element_type=F32,
                )
                own[e % 2, which] = value[:half]
                sent[e, which] = value[half:].astype(BF16)
            pre_copies[e].start()

        def activate(e):
            pre_copies[e].wait_recv()
            gate_sum = own[e % 2, 0] + got[e, 0].astype(F32)
            up_sum = own[e % 2, 1] + got[e, 1].astype(F32)
            value = gate_sum / (1.0 + jnp.exp(-gate_sum)) * up_sum
            hidden[e, pl.ds(0, half)] = value.astype(BF16)
            hid_copies[e].start()

        def answer(e):
            load_out(e).wait()
            hid_copies[e].wait_recv()

            @pl.loop(0, cols // tile)
            def _(step):
                start = pl.multiple_of(step * tile, tile)
                value = jnp.dot(
                    hidden[e],
                    out_weights[e % 2, :, pl.ds(start, tile)],
                    preferred_element_type=F32,
                )
                mixture[:, pl.ds(start, tile)] += route_ref[:, e : e + 1] * value.astype(
                    BF16
                ).astype(F32)

            if e + 2 < count:
                load_out(e + 2).start()

        for e in range(count):
            project(e)
            if e >= 1:
                activate(e - 1)
            if e >= 2:
                answer(e - 2)
        activate(count - 1)
        if count >= 2:
            answer(count - 2)
        answer(count - 1)

        for place in range(sources):
            mixed[place] = mixture[pl.ds(place * block, block)].astype(BF16)
        turn = side * (sources // 2)
        back_copies = []
        for at, peer in enumerate(peers):
            copy = pltpu.make_async_remote_copy(
                src_ref=mixed.at[lax.rem(peer + turn, sources)],
                dst_ref=back_ref.at[me],
                send_sem=back_send.at[at],
                recv_sem=back_recv.at[at],
                device_id={"expert": peer},
                device_id_type=mesh_ids,
            )
            copy.start()
            back_copies.append(copy)
        back_ref[me] = mixed[lax.rem(me + turn, sources)]
        for e in range(count):
            pre_copies[e].wait_send()
            hid_copies[e].wait_send()
        for copy in back_copies:
            copy.wait()

    semaphores = pltpu.SemaphoreType.DMA
    in_vmem = pl.BlockSpec(memory_space=pltpu.VMEM)
    in_place = pl.BlockSpec(memory_space=pl.ANY)
    return pl.pallas_call(
        kernel,
        out_shape=jax.ShapeDtypeStruct((sources, block, cols), BF16),
        in_specs=[in_vmem] * 4 + [in_place] * 3,
        out_specs=in_vmem,
        scratch_shapes=[
            pltpu.VMEM(low_sent.shape, BF16),
            pltpu.VMEM((2, 2, depth, ffw), BF16),
            pltpu.VMEM((2, ffw, cols), BF16),
            pltpu.VMEM((2, total, ffw), F32),
            pltpu.VMEM((2, 2, half, ffw), F32),
            pltpu.VMEM((count, 2, half, ffw), BF16),
            pltpu.VMEM((count, 2, half, ffw), BF16),
            pltpu.VMEM((count, total, ffw), BF16),
            pltpu.VMEM((total, cols), F32),
            pltpu.VMEM((sources, block, cols), BF16),
            semaphores((2, 2)),
            semaphores((2,)),
            semaphores((sources - 1,)),
            semaphores((sources - 1,)),
            semaphores((count,)),
            semaphores((count,)),
            semaphores((count,)),
            semaphores((count,)),
            semaphores((sources - 1,)),
            semaphores((sources - 1,)),
        ],
        compiler_params=pltpu.CompilerParams(
            collective_id=5, has_side_effects=True, vmem_limit_bytes=44 << 20
        ),
    )(rows, low_sent, right, route, gate, up, down)


def shards(
    inputs,
    attn_gain,
    qkv_weight,
    out_weight,
    cache,
    lengths,
    moe_gain,
    router_weight,
    expert_ids,
    gate_weight,
    up_weight,
    down_weight,
    pool_left,
    pool_right,
    pair_slot,
):
    steps, rows_here, width = inputs.shape
    experts_here, part_cols, ffw = gate_weight.shape
    slots_here, _, _, rank = pool_left.shape
    right_cols = pool_right.shape[3]
    lat = cache.shape[2]
    span_here = cache.shape[1]
    shard_count = lax.axis_size("expert")
    shard_index = lax.axis_index("expert")
    tensor_count = lax.axis_size("tensor")
    tensor_index = lax.axis_index("tensor")
    expert_count = shard_count * experts_here
    col_start = tensor_index * part_cols
    batch = steps * rows_here
    total_rows = shard_count * batch
    score_scale = lat ** (-0.5)
    paired = tensor_count == 2

    own_slots = shard_index * slots_here + jnp.arange(slots_here, dtype=jnp.int32)
    serves = (pair_slot[:, None] == own_slots[None, :]).astype(BF16)

    piece_cols = right_cols // tensor_count
    right_piece = lax.dynamic_slice_in_dim(pool_right, tensor_index * piece_cols, piece_cols, 3)
    right_sent = jnp.einsum(
        "es,sxrf->exrf", serves, right_piece, preferred_element_type=F32
    ).astype(BF16)
    right_sent = right_sent.reshape(shard_count, experts_here * 2 * rank, piece_cols)

    chosen = jnp.any(
        expert_ids.reshape(batch, -1)[:, :, None]
        == jnp.arange(expert_count, dtype=jnp.int32)[None, None, :],
        axis=1,
    ).astype(F32)

    tokens = inputs.reshape(batch, width)
    tokens_wide = tokens.astype(F32)
    square_mean = jnp.mean(tokens_wide * tokens_wide, axis=-1, keepdims=True)
    token_cols = lax.dynamic_slice_in_dim(tokens, col_start, part_cols, 1)
    gain_piece = lax.dynamic_slice_in_dim(attn_gain, col_start, part_cols, 0)
    normed_cols = (
        token_cols.astype(F32) * lax.rsqrt(square_mean + EPS) * gain_piece
    ).astype(BF16)
    projected = jnp.dot(normed_cols, qkv_weight, preferred_element_type=F32)
    projected_all, right_got = exchange(
        [
            (projected, ("tensor",), "gather"),
            (right_sent, ("expert",), "scatter"),
        ],
        0,
        ("expert", "tensor"),
    )
    projected = jnp.sum(projected_all, axis=0)
    right_own = jnp.sum(right_got.astype(F32), axis=0).astype(BF16)
    right_own = right_own.reshape(experts_here, 2, rank, piece_cols)
    right_full = lax.all_gather(right_own, ("dp", "tensor"), axis=3, tiled=True)
    queries = projected[:, :lat].astype(BF16).reshape(steps, rows_here, lat)
    fresh = projected[:, lat:].astype(BF16).reshape(steps, rows_here, lat)

    positions = tensor_index * span_here + jnp.arange(span_here, dtype=jnp.int32)
    visible = (positions[None, :] < lengths[:, None])[:, None, :]
    scores = (
        jnp.einsum("sbl,bpl->bsp", queries, cache, preferred_element_type=F32) * score_scale
    )
    local_top = jnp.max(jnp.where(visible, scores, FLOOR), axis=-1, keepdims=True)
    weights = jnp.where(visible, jnp.exp(scores - local_top), 0.0)
    terms = jnp.concatenate(split_terms(weights, 3), axis=1)
    sums = jnp.einsum("bmp,bpl->bml", terms, cache, preferred_element_type=F32)
    sums = jnp.sum(sums.reshape(rows_here, 3, steps, lat), axis=1)
    local_total = jnp.sum(weights, axis=-1, keepdims=True)
    packed = jnp.concatenate(
        (
            sums,
            jnp.broadcast_to(local_top, (rows_here, steps, 64)),
            jnp.broadcast_to(local_total, (rows_here, steps, 64)),
        ),
        axis=2,
    )
    packed = packed.reshape(rows_here * steps, lat + 128)
    parts = exchange([(packed, ("tensor",), "gather")], 1)[0]
    parts = parts.reshape(tensor_count, rows_here, steps, lat + 128)
    part_sums, part_tops, part_totals = (
        parts[..., :lat],
        parts[..., lat],
        parts[..., lat + 64],
    )

    fresh_wide = fresh.astype(F32)
    latest = (
        jnp.sum(queries.astype(F32)[:, None] * fresh_wide[None], axis=-1) * score_scale
    )
    step_range = jnp.arange(steps)
    usable = (step_range[None, :] <= step_range[:, None])[:, :, None]
    latest_top = jnp.max(jnp.where(usable, latest, FLOOR), axis=1)
    highest = jnp.maximum(jnp.max(part_tops, axis=0), latest_top.T)
    factors = jnp.exp(part_tops - highest[None])
    latest_weights = jnp.where(usable, jnp.exp(latest - highest.T[:, None, :]), 0.0)
    denominator = jnp.sum(part_totals * factors, axis=0) + jnp.sum(latest_weights, axis=1).T
    numerator = jnp.sum(part_sums * factors[..., None], axis=0).transpose(1, 0, 2) + jnp.sum(
        latest_weights[..., None] * fresh_wide[None], axis=1
    )
    attended = (numerator / denominator.T[..., None]).astype(BF16).reshape(batch, lat)
    middle = (
        token_cols.astype(F32) + jnp.dot(attended, out_weight, preferred_element_type=F32)
    ).astype(BF16)

    gain_cols = lax.dynamic_slice_in_dim(moe_gain, col_start, part_cols, 0)
    router_rows = lax.dynamic_slice_in_dim(router_weight, col_start, part_cols, 0).astype(F32)
    middle_wide = middle.astype(F32)
    partial_logits = jnp.dot(
        middle_wide * gain_cols, router_rows, precision=lax.Precision.HIGHEST
    )
    partial_squares = jnp.sum(middle_wide * middle_wide, axis=-1, keepdims=True)
    statistics = jnp.concatenate(
        (
            partial_logits,
            jnp.where(tensor_index == 0, chosen, 0.0),
            jnp.broadcast_to(partial_squares, (batch, 128 - 2 * expert_count)),
        ),
        axis=1,
    )
    statistics, middle_all = exchange(
        [(statistics, ("expert", "tensor"), "gather"), (middle, ("expert",), "gather")], 2
    )
    statistics = jnp.sum(
        statistics.reshape(shard_count, tensor_count, batch, 128), axis=1
    )

    def turned(value):
        if not paired:
            return value
        half = shard_count // 2
        swapped = jnp.concatenate((value[half:], value[:half]), axis=0)
        return jnp.where(tensor_index == 0, value, swapped)

    statistics = turned(statistics).reshape(total_rows, 128)
    rows_all = turned(middle_all).reshape(total_rows, part_cols)
    mask_all = statistics[:, expert_count : 2 * expert_count]

    inverse = lax.rsqrt(statistics[:, 127:] / width + EPS)
    routed_in = (rows_all.astype(F32) * inverse * gain_cols).astype(BF16)
    gated = jax.nn.sigmoid(inverse * statistics[:, :expert_count]) * mask_all
    route = (ROUTE_SCALE * gated / jnp.sum(gated, axis=-1, keepdims=True)).astype(BF16)
    route_here = lax.dynamic_slice_in_dim(
        route, shard_index * experts_here, experts_here, 1
    ).astype(F32)

    low = jnp.einsum("nd,sxdr->snxr", routed_in, pool_left, preferred_element_type=F32)
    low = low.astype(BF16).reshape(slots_here, total_rows, 2 * rank)
    low_sent = jnp.einsum("es,snq->enq", serves, low, preferred_element_type=F32).astype(BF16)
    low_sent = low_sent.reshape(shard_count, experts_here * total_rows, 2 * rank)
    if paired:
        returned = expert_stage(
            routed_in, low_sent, right_full, route_here, gate_weight, up_weight, down_weight
        )
    else:
        low_got = exchange([(low_sent, ("expert",), "scatter")], 3)[0]
        low_own = jnp.sum(low_got.astype(F32), axis=0).astype(BF16)
        low_own = low_own.reshape(experts_here, total_rows, 2, rank)
        mixture = jnp.zeros((total_rows, part_cols), F32)
        for expert in range(experts_here):
            partial = [
                jnp.dot(routed_in, weight[expert], preferred_element_type=F32)
                + jnp.dot(
                    low_own[expert, :, which],
                    right_full[expert, which],
                    preferred_element_type=F32,
                )
                for which, weight in enumerate((gate_weight, up_weight))
            ]
            summed = lax.psum_scatter(
                jnp.concatenate(partial, axis=1), "tensor", scatter_dimension=0, tiled=True
            )
            hidden = (jax.nn.silu(summed[:, :ffw]) * summed[:, ffw:]).astype(BF16)
            hidden = lax.all_gather(hidden, "tensor", axis=0, tiled=True)
            answered = jnp.dot(hidden, down_weight[expert], preferred_element_type=F32)
            weight = route_here[:, expert : expert + 1]
            mixture = mixture + weight * answered.astype(BF16).astype(F32)
        returned = mixture.astype(BF16).reshape(shard_count, batch, part_cols)
        returned = exchange([(returned, ("expert",), "scatter")], 4)[0]
    outputs = (middle_wide + jnp.sum(returned.astype(F32), axis=0)).astype(BF16)
    return outputs.reshape(steps, rows_here, part_cols)


def solution(mesh):
    return jax.shard_map(
        shards,
        mesh=mesh,
        in_specs=(
            P(None, ("groups", "expert", "dp"), None),
            P(),
            P("tensor", None),
            P(None, "tensor"),
            P(("groups", "expert", "dp"), "tensor", None),
            P(("groups", "expert", "dp")),
            P(),
            P(),
            P(None, ("groups", "expert", "dp"), None),
            P("expert", "tensor", None),
            P("expert", "tensor", None),
            P("expert", None, "tensor"),
            P(("groups", "expert"), None, "tensor", None),
            P(("groups", "expert"), None, None, "dp"),
            P("groups"),
        ),
        out_specs=P(None, ("groups", "expert", "dp"), "tensor"),
        check_vma=False,
    )
```
